32 devices in a mesh: row: 8 (over y, x, core), col: 4 (over z).
Axes of the slice: x: 2, y: 2, z: 4, core: 2. Of those that a mesh axis runs over, the one named last changes fastest.
Arguments:
- probes: bfloat16 [8, 1024, 256], P('row', 'col'), may hold values from -6 to 6
- kernel_spectra: bfloat16 [2, 1024, 1024, 256], P(None, 'row', 'col'), may hold values from -0.25 to 0.25
- sensor_mask: int32 [1024], P('row'), may hold values 0 or 1
- precision: float32 [1024], P('row'), may hold values from 0.25 to 4
- source_block: int32 [1024], P('col'), may hold values from 0 to 15
- damping: float32 [16], replicated, may hold values from 0.2 to 2
Outputs:
- hessian_product: float32 [8, 1024, 256], P('row', 'col')
The draws below stay inside these ranges and needn't reach their ends.
Inputs may be any that keep to these rules, and one draw needn't show every extreme that they name: `sensor_mask`: 1 marks a sensor whose records count. `source_block`: each entry names one of the 16 damping groups.
All inputs are finite; a program needn't handle non-finite values. No bound on the sum of `sensor_mask` on one device may be relied on, other than what follows from the above.
Results may differ from the reference program's by a relative error of at most 0.023.
Values may be sent and summed in bfloat16 or wider, within the bound.
A program may use at most 256 MiB of HBM per device.

```python
import math
import jax
import jax.numpy as jnp
from jax import lax

NSRC = 1024
NSENS = 1024
TIMES = 256
NBLOCK = 16
NPROBE = 8
N_ROW = 8
N_COL = 4


def with_ends(entries, own_key, low, high):
    spot = [jax.random.randint(jax.random.fold_in(own_key, axis), (), 0, length) for axis, length in enumerate(entries.shape)]
    longest = entries.shape.index(max(entries.shape))
    neighbour = spot[:longest] + [(spot[longest] + 1) % entries.shape[longest]] + spot[longest + 1:]
    return entries.at[tuple(spot)].set(low).at[tuple(neighbour)].set(high)


def levels(stream_key, extent, split, low, high):
    def one(axis_at, blocks):
        heights = jax.random.uniform(jax.random.fold_in(jax.random.fold_in(stream_key, 6), axis_at), (blocks,), jnp.float32, low / len(split), high / len(split))
        return jnp.repeat(jnp.exp(heights), extent[axis_at] // blocks).reshape((-1,) + (1,) * (len(extent) - axis_at - 1))

    factor_of = one(*split[0])
    for cut in split[1:]:
        factor_of = factor_of * one(*cut)
    return factor_of


def centred(stream_key, dims, scale, reach, pieces=(), held_as=jnp.bfloat16):
    values = jax.random.normal(stream_key, dims, jnp.float32) * scale
    if len(pieces) > 0:
        values = levels(stream_key, dims, pieces, -0.22, 0.18) * values
    return jnp.clip(values, min=-reach, max=reach).astype(held_as)


def setup_inputs(seed: int = 0) -> dict:
    arg_keys = jax.random.split(jax.random.key(seed), 7)
    probes = centred(arg_keys[0], (NPROBE, NSRC, TIMES), 1.0, 6.0, ((0, 8), (1, 4)))
    kernel_spectra = centred(arg_keys[1], (2, NSENS, NSRC, TIMES), (NSRC // 2) ** -0.5, 0.25, ((1, 8), (2, 4)))
    sensor_mask = with_ends((jax.random.randint(arg_keys[2], (NSENS,), 0, 4) < 3).astype(jnp.int32), jax.random.fold_in(arg_keys[2], 1), 0, 1)
    precision = jnp.clip(jnp.exp(math.log(4.0) - 2.7725887 * jax.random.uniform(arg_keys[3], (NSENS,), jnp.float32) ** levels(arg_keys[3], (NSENS,), ((0, 8),), -0.2, 0.2)), 0.25, 4.0)
    source_block = with_ends(jax.random.randint(arg_keys[4], (NSRC,), 0, NBLOCK), jax.random.fold_in(arg_keys[4], 1), 0, NBLOCK - 1).astype(jnp.int32)
    damping = jnp.clip(jnp.exp(jax.random.uniform(arg_keys[5], (NBLOCK,), jnp.float32, math.log(0.2), math.log(2.0))), 0.2, 2.0)
    return {"probes": probes, "kernel_spectra": kernel_spectra, "sensor_mask": sensor_mask, "precision": precision, "source_block": source_block, "damping": damping}


def dft_tables(length):
    period = 2 * length
    positions = jnp.arange(length, dtype=jnp.int32)
    phases = (positions[:, None] * positions[None, :]) % period
    angles = phases.astype(jnp.float32) * (2.0 * math.pi / period)
    cosine = jnp.cos(angles)
    sines = jnp.sin(angles)
    weight = jnp.where(positions == 0, 1.0, 2.0).astype(jnp.float32) / period
    forward = jnp.concatenate([cosine, -sines], axis=1).astype(jnp.bfloat16)
    inverse = jnp.concatenate([cosine * weight[:, None], -sines * weight[:, None]], axis=0).astype(jnp.bfloat16)
    return forward, inverse


def transform(block, table):
    dims_in = block.shape
    flattened = block.reshape(-1, dims_in[-1])
    result = jnp.dot(flattened, table, preferred_element_type=jnp.float32)
    return result.reshape(dims_in[:-1] + (table.shape[1],))


def mix(form, left, right):
    return jnp.einsum(form, left.astype(jnp.float32), right.astype(jnp.float32), precision=lax.Precision.HIGHEST)


def freq_forward(kernel, spectra):
    freq_count = kernel.shape[3]
    s_real = spectra[..., :freq_count]
    s_imag = spectra[..., freq_count:]
    out_real = mix("rsf,psf->prf", kernel[0], s_real) - mix("rsf,psf->prf", kernel[1], s_imag)
    out_imag = mix("rsf,psf->prf", kernel[0], s_imag) + mix("rsf,psf->prf", kernel[1], s_real)
    return jnp.concatenate([out_real, out_imag], axis=-1)


def freq_adjoint(kernel, spectra):
    freq_count = kernel.shape[3]
    y_real = spectra[..., :freq_count]
    y_imag = spectra[..., freq_count:]
    g_real = mix("rsf,prf->psf", kernel[0], y_real) + mix("rsf,prf->psf", kernel[1], y_imag)
    g_imag = mix("rsf,prf->psf", kernel[0], y_imag) - mix("rsf,prf->psf", kernel[1], y_real)
    return jnp.concatenate([g_real, g_imag], axis=-1)


def reference(probes, kernel_spectra, sensor_mask, precision, source_block, damping):
    forward, inverse = dft_tables(TIMES)
    src_size = NSRC // N_COL
    sens_size = NSENS // N_ROW

    def forward_block(block, total):
        first_row = block.astype(jnp.int32) * src_size
        history = lax.dynamic_slice_in_dim(probes, first_row, src_size, 1)
        spectra = transform(history, forward).astype(jnp.bfloat16)
        kernel_part = lax.dynamic_slice_in_dim(kernel_spectra, first_row, src_size, 2)
        block_spec = freq_forward(kernel_part, spectra).astype(jnp.bfloat16)
        return total + transform(block_spec, inverse)

    predicted = lax.fori_loop(0, N_COL, forward_block, jnp.zeros((NPROBE, NSENS, TIMES), jnp.float32))
    record_weight = jnp.where(sensor_mask == 1, precision, jnp.zeros_like(precision))
    weighted = (predicted * record_weight[None, :, None]).astype(jnp.bfloat16)
    residual_spec = transform(weighted, inverse.T).astype(jnp.bfloat16)

    def backward_block(block, total):
        first_row = block.astype(jnp.int32) * sens_size
        picked = lax.dynamic_slice_in_dim(residual_spec, first_row, sens_size, 1)
        kernel_part = lax.dynamic_slice_in_dim(kernel_spectra, first_row, sens_size, 1)
        block_grad = freq_adjoint(kernel_part, picked).astype(jnp.bfloat16)
        return total + transform(block_grad, forward.T)

    summed = lax.fori_loop(0, N_ROW, backward_block, jnp.zeros((NPROBE, NSRC, TIMES), jnp.float32))
    source_damping = damping[source_block]
    return summed + source_damping[None, :, None] * probes.astype(jnp.float32)
```

```python
import functools
import math

import jax
import jax.numpy as jnp
import ml_dtypes
import numpy as np
from jax import lax
from jax.experimental import pallas as pl
from jax.experimental.pallas import tpu as pltpu
from jax.sharding import PartitionSpec as P

GROUP = 16
NT = (((1,), (1,)), ((), ()))
TN = (((0,), (0,)), ((), ()))


def dft_tables(length):
    period = 2 * length
    positions = np.arange(length)
    phases = positions[:, None] * positions[None, :] % period
    angles = phases * (2.0 * math.pi / period)
    cosine = np.cos(angles).astype(np.float32)
    sines = np.sin(angles).astype(np.float32)
    weight = (np.where(positions == 0, 1.0, 2.0) / period).astype(np.float32)
    forward = np.concatenate([cosine, -sines], axis=1).astype(ml_dtypes.bfloat16)
    inverse = np.concatenate([cosine * weight[:, None], -sines * weight[:, None]], axis=0).astype(
        ml_dtypes.bfloat16
    )
    return (forward, inverse)


def dot(a, b, dims=None):
    if dims is None:
        return jnp.dot(a, b, preferred_element_type=jnp.float32)
    return lax.dot_general(a, b, dims, preferred_element_type=jnp.float32)


def forward_kernel(k_ref, probes_ref, fwd_t_ref, inv_t_ref, kt_ref, pred_ref, x_ref, e_ref):
    step = pl.program_id(0)
    _, rows, sources, freqs = k_ref.shape
    groups = freqs // GROUP
    nprobe = probes_ref.shape[0]
    columns = nprobe * 2 * GROUP

    @pl.when(step == 0)
    def _():
        for p in range(nprobe):
            spec = dot(fwd_t_ref[...], probes_ref[p], NT).astype(jnp.bfloat16)
            real = spec[:freqs].reshape(groups, GROUP, sources)
            imag = spec[freqs:].reshape(groups, GROUP, sources)
            at = p * 2 * GROUP
            x_ref[:, 0, at : at + GROUP, :] = real
            x_ref[:, 0, at + GROUP : at + 2 * GROUP, :] = imag
            x_ref[:, 1, at : at + GROUP, :] = -imag
            x_ref[:, 1, at + GROUP : at + 2 * GROUP, :] = real

    def turn(r, carry):
        for k in range(2):
            kt_ref[:, k, r, :, :] = k_ref[k, r].T.reshape(groups, GROUP, sources)
        return carry

    lax.fori_loop(0, rows, turn, 0, unroll=2)

    own = lax.broadcasted_iota(jnp.int32, (rows * GROUP, columns), 0) % GROUP
    col = lax.broadcasted_iota(jnp.int32, (rows * GROUP, columns), 1) % GROUP
    keep = own == col
    pick_row = lax.broadcasted_iota(jnp.int32, (rows, rows * GROUP), 0)
    pick_col = lax.broadcasted_iota(jnp.int32, (rows, rows * GROUP), 1) // GROUP
    pick = (pick_row == pick_col).astype(jnp.bfloat16)
    at_row = pl.ds(pl.multiple_of(step * rows, rows), rows)
    for g in range(groups):
        left = kt_ref[g].reshape(2, rows * GROUP, sources)
        out = dot(left[0], x_ref[g, 0], NT) + dot(left[1], x_ref[g, 1], NT)
        kept = jnp.where(keep, out, 0.0).astype(jnp.bfloat16)
        e_ref[at_row, g * columns : (g + 1) * columns] = dot(pick, kept).astype(jnp.bfloat16)

    @pl.when(step == pl.num_programs(0) - 1)
    def _():
        sensors = e_ref.shape[0]
        turned = e_ref[...].T.reshape(groups, nprobe, 2, GROUP, sensors)
        for p in range(nprobe):
            spec = jnp.concatenate(
                [turned[:, p, k].reshape(freqs, sensors) for k in range(2)], axis=0
            )
            pred_ref[p] = dot(inv_t_ref[...], spec).astype(jnp.bfloat16)


def adjoint_kernel(kt_ref, weighted_ref, inv_ref, syn_ref, out_ref, y_ref, g_ref):
    g = pl.program_id(0)
    sensors = weighted_ref.shape[2]
    nprobe = weighted_ref.shape[0]
    freqs = inv_ref.shape[0] // 2
    groups = freqs // GROUP
    sources = kt_ref.shape[-1]
    columns = nprobe * 2 * GROUP

    @pl.when(g == 0)
    def _():
        for p in range(nprobe):
            spec = dot(inv_ref[...], weighted_ref[p]).astype(jnp.bfloat16)
            for k in range(2):
                at = (2 * p + k) * GROUP
                y_ref[:, at : at + GROUP, :] = spec[k * freqs : (k + 1) * freqs].reshape(
                    groups, GROUP, sensors
                )

    part = 16
    width = part * GROUP
    own = lax.broadcasted_iota(jnp.int32, (columns, width), 0) % GROUP
    col = lax.broadcasted_iota(jnp.int32, (columns, width), 1) % GROUP
    keep = own == col
    spread_row = lax.broadcasted_iota(jnp.int32, (sensors, sensors * GROUP), 0)
    spread_col = lax.broadcasted_iota(jnp.int32, (sensors, sensors * GROUP), 1) // GROUP
    spread = (spread_row == spread_col).astype(jnp.bfloat16)
    y = y_ref[g]
    wide = []
    for n in range(sensors // part):
        piece = dot(y, spread[:, n * width : (n + 1) * width])
        wide.append(jnp.where(keep, piece, 0.0).astype(jnp.bfloat16))
    wide = jnp.concatenate(wide, axis=1)
    sums = [dot(wide, kt_ref[0, k].reshape(sensors * GROUP, sources)) for k in range(2)]
    real, imag = [s.reshape(nprobe, 2, GROUP, sources) for s in sums]
    at = pl.ds(pl.multiple_of(g * GROUP, GROUP), GROUP)
    late = pl.ds(pl.multiple_of(freqs + g * GROUP, GROUP), GROUP)
    g_ref[:, at, :] = (real[:, 0] + imag[:, 1]).astype(jnp.bfloat16)
    g_ref[:, late, :] = (real[:, 1] - imag[:, 0]).astype(jnp.bfloat16)

    @pl.when(g == pl.num_programs(0) - 1)
    def _():
        for p in range(nprobe):
            out_ref[p] = dot(g_ref[p], syn_ref[...], TN).astype(jnp.bfloat16)


def whole(shape):
    return pl.BlockSpec(shape, lambda i: (0,) * len(shape))


def forward_call(kernel_spectra, probes, fwd_t, inv_t):
    _, sensors, sources, freqs = kernel_spectra.shape
    nprobe, _, times = probes.shape
    groups = freqs // GROUP
    columns = nprobe * 2 * GROUP
    rows = 16
    return pl.pallas_call(
        forward_kernel,
        grid=(sensors // rows,),
        in_specs=[
            pl.BlockSpec((2, rows, sources, freqs), lambda i: (0, i, 0, 0)),
            whole(probes.shape),
            whole(fwd_t.shape),
            whole(inv_t.shape),
        ],
        out_specs=[
            pl.BlockSpec((groups, 2, rows, GROUP, sources), lambda i: (0, 0, i, 0, 0)),
            whole((nprobe, times, sensors)),
        ],
        out_shape=[
            jax.ShapeDtypeStruct((groups, 2, sensors, GROUP, sources), jnp.bfloat16),
            jax.ShapeDtypeStruct((nprobe, times, sensors), jnp.bfloat16),
        ],
        scratch_shapes=[
            pltpu.VMEM((groups, 2, columns, sources), jnp.bfloat16),
            pltpu.VMEM((sensors, groups * columns), jnp.bfloat16),
        ],
        compiler_params=pltpu.CompilerParams(vmem_limit_bytes=56 * 1024 * 1024),
        name="forward",
    )(kernel_spectra, probes, fwd_t, inv_t)


def adjoint_call(turned, weighted, inverse, synthesis):
    groups, _, sensors, _, sources = turned.shape
    nprobe, times, _ = weighted.shape
    freqs = groups * GROUP
    columns = nprobe * 2 * GROUP
    return pl.pallas_call(
        adjoint_kernel,
        grid=(groups,),
        in_specs=[
            pl.BlockSpec((1, 2, sensors, GROUP, sources), lambda i: (i, 0, 0, 0, 0)),
            whole(weighted.shape),
            whole(inverse.shape),
            whole(synthesis.shape),
        ],
        out_specs=whole((nprobe, sources, times)),
        out_shape=jax.ShapeDtypeStruct((nprobe, sources, times), jnp.bfloat16),
        scratch_shapes=[
            pltpu.VMEM((groups, columns, sensors), jnp.bfloat16),
            pltpu.VMEM((nprobe, 2 * freqs, sources), jnp.bfloat16),
        ],
        compiler_params=pltpu.CompilerParams(vmem_limit_bytes=56 * 1024 * 1024),
        name="adjoint",
    )(turned, weighted, inverse, synthesis)


def plain_forward(kernel_spectra, probes, fwd_t, inv_t):
    freqs = kernel_spectra.shape[3]
    spec = jnp.einsum("Ft,pst->psF", fwd_t, probes, preferred_element_type=jnp.float32)
    spec = spec.astype(jnp.bfloat16)
    spec = spec.reshape(spec.shape[:2] + (2, freqs))
    a = jnp.einsum("krsf,psjf->kjprf", kernel_spectra, spec, preferred_element_type=jnp.float32)
    both = jnp.concatenate([a[0, 0] - a[1, 1], a[0, 1] + a[1, 0]], axis=-1).astype(jnp.bfloat16)
    pred = jnp.einsum("tF,prF->ptr", inv_t, both, preferred_element_type=jnp.float32)
    return kernel_spectra, pred.astype(jnp.bfloat16)


def plain_adjoint(kernel_spectra, weighted, inverse, synthesis):
    freqs = kernel_spectra.shape[3]
    spec = jnp.einsum("Ft,ptr->prF", inverse, weighted, preferred_element_type=jnp.float32)
    spec = spec.astype(jnp.bfloat16)
    spec = spec.reshape(spec.shape[:2] + (2, freqs))
    a = jnp.einsum("krsf,prjf->kjpsf", kernel_spectra, spec, preferred_element_type=jnp.float32)
    both = jnp.concatenate([a[0, 0] + a[1, 1], a[0, 1] - a[1, 0]], axis=-1).astype(jnp.bfloat16)
    out = jnp.einsum("psF,Ft->pst", both, synthesis, preferred_element_type=jnp.float32)
    return out.astype(jnp.bfloat16)


def body(probes, kernel_spectra, sensor_mask, precision, source_block, damping):
    forward, inverse = dft_tables(probes.shape[2])
    fwd_t, inv_t = jnp.asarray(forward.T), jnp.asarray(inverse.T)
    inverse = jnp.asarray(inverse)
    _, sensors, sources, freqs = kernel_spectra.shape
    tiled = sensors % 128 == 0 and sources % 128 == 0 and freqs % 128 == 0
    run_forward = forward_call if tiled else plain_forward
    run_adjoint = adjoint_call if tiled else plain_adjoint

    gathered = lax.all_gather(probes, "row", axis=0, tiled=True)
    turned, pred = run_forward(kernel_spectra, gathered, fwd_t, inv_t)
    record_weight = jnp.where(sensor_mask == 1, precision, jnp.zeros_like(precision))
    predicted = lax.psum_scatter(pred, "col", scatter_dimension=0, tiled=True)
    weighted = (predicted.astype(jnp.float32) * record_weight[None, None, :]).astype(jnp.bfloat16)
    weighted = lax.all_gather(weighted, "col", axis=0, tiled=True)
    part = run_adjoint(turned, weighted, inverse, fwd_t)
    summed = lax.psum_scatter(part, "row", scatter_dimension=0, tiled=True).astype(jnp.float32)
    groups = jnp.arange(damping.shape[0], dtype=jnp.int32)
    one_hot = (source_block[:, None] == groups[None, :]).astype(jnp.float32)
    source_damping = jnp.dot(one_hot, damping, precision=lax.Precision.HIGHEST)
    return summed + source_damping[None, :, None] * probes.astype(jnp.float32)


def solution(mesh):
    placed = (P("row", "col", None), P(None, "row", "col", None), P("row"), P("row"), P("col"), P())
    return jax.shard_map(
        body, mesh=mesh, in_specs=placed, out_specs=P("row", "col", None), check_vma=False
    )
```

```python
import functools
import math

import jax
import jax.numpy as jnp
import ml_dtypes
import numpy as np
from jax import lax
from jax.experimental import pallas as pl
from jax.experimental.pallas import tpu as pltpu
from jax.sharding import PartitionSpec as P

GROUP = 16
HALVES = 2
MESH = pl.DeviceIdType.MESH
NT = (((1,), (1,)), ((), ()))
TN = (((0,), (0,)), ((), ()))


def dft_tables(length):
    period = 2 * length
    positions = np.arange(length)
    phases = positions[:, None] * positions[None, :] % period
    angles = phases * (2.0 * math.pi / period)
    cosine = np.cos(angles).astype(np.float32)
    sines = np.sin(angles).astype(np.float32)
    weight = (np.where(positions == 0, 1.0, 2.0) / period).astype(np.float32)
    forward = np.concatenate([cosine, -sines], axis=1).astype(ml_dtypes.bfloat16)
    inverse = np.concatenate([cosine * weight[:, None], -sines * weight[:, None]], axis=0).astype(
        ml_dtypes.bfloat16
    )
    return (forward, inverse)


def dot(a, b, dims=None):
    if dims is None:
        return jnp.dot(a, b, preferred_element_type=jnp.float32)
    return lax.dot_general(a, b, dims, preferred_element_type=jnp.float32)


def fused_kernel(
    n_row,
    n_col,
    halves,
    k_hbm,
    probes_ref,
    weight_ref,
    fwd_t_ref,
    inv_ref,
    pick_ref,
    out_ref,
    stage,
    kt_ref,
    gath,
    x_ref,
    et_ref,
    pred_ref,
    pred_in,
    wt_ref,
    y_ref,
    acc_ref,
    g_ref,
    hess_out,
    hess_in,
    k_sem,
    gs_sem,
    gr_sem,
    ps_sem,
    pr_sem,
    ws_sem,
    wr_sem,
    hs_sem,
    hr_sem,
):
    me_row, me_col = lax.axis_index("row"), lax.axis_index("col")
    _, sensors, sources, freqs = k_hbm.shape
    nloc = probes_ref.shape[0]
    nprobe = nloc * n_row
    nown = nprobe // n_col
    groups = freqs // GROUP
    columns = nprobe * 2 * GROUP
    rows = stage.shape[2]
    steps = sensors // rows
    half = sensors // halves

    def row_peer(d):
        return lax.rem(me_row + d, n_row)

    def col_peer(d):
        return lax.rem(me_col + d, n_col)

    def load(step, slot):
        at = pl.ds(pl.multiple_of(step * rows, rows), rows)
        return pltpu.make_async_copy(k_hbm.at[:, at], stage.at[slot], k_sem.at[slot])

    for slot in range(2):
        load(slot, slot).start()

    barrier = pltpu.get_barrier_semaphore()
    for d in range(1, n_row):
        pl.semaphore_signal(barrier, inc=1, device_id=(row_peer(d), me_col), device_id_type=MESH)
    for d in range(1, n_col):
        pl.semaphore_signal(barrier, inc=1, device_id=(me_row, col_peer(d)), device_id_type=MESH)
    pl.semaphore_wait(barrier, n_row + n_col - 2)

    def send(src, dst, send_sem, recv_sem, device):
        return pltpu.make_async_remote_copy(
            src_ref=src,
            dst_ref=dst,
            send_sem=send_sem,
            recv_sem=recv_sem,
            device_id=device,
            device_id_type=MESH,
        )

    gathers = []
    for d in range(1, n_row):
        copy = send(
            probes_ref,
            gath.at[d],
            gs_sem.at[d],
            gr_sem.at[d],
            (row_peer(d), me_col),
        )
        copy.start()
        gathers.append(copy)

    def turn_step(step, carry):
        slot = lax.rem(step, 2)
        load(step, slot).wait()

        def turn(r, inner):
            for k in range(2):
                kt_ref[:, k, step * rows + r, :, :] = stage[slot, k, r].T.reshape(
                    groups, GROUP, sources
                )
            return inner

        lax.fori_loop(0, rows, turn, 0, unroll=2)

        @pl.when(step + 2 < steps)
        def _():
            load(step + 2, slot).start()

        return carry

    lax.fori_loop(0, steps, turn_step, 0)

    def spectra(p, block):
        spec = dot(fwd_t_ref[...], block, NT).astype(jnp.bfloat16)
        real = spec[:freqs].reshape(groups, GROUP, sources)
        imag = spec[freqs:].reshape(groups, GROUP, sources)
        first = pl.ds(pl.multiple_of(p * 2 * GROUP, GROUP), GROUP)
        second = pl.ds(pl.multiple_of(p * 2 * GROUP + GROUP, GROUP), GROUP)
        x_ref[:, 0, first, :] = real
        x_ref[:, 0, second, :] = imag
        x_ref[:, 1, first, :] = -imag
        x_ref[:, 1, second, :] = real

    for j in range(nloc):
        spectra(me_row * nloc + j, probes_ref[j])
    for d in range(1, n_row):
        gathers[d - 1].wait_recv()
        origin = lax.rem(me_row + n_row - d, n_row)
        for j in range(nloc):
            spectra(origin * nloc + j, gath[d, j])

    own = lax.broadcasted_iota(jnp.int32, (1, GROUP, columns), 1)
    col = lax.broadcasted_iota(jnp.int32, (1, GROUP, columns), 2) % GROUP
    keep = own == col
    own = lax.broadcasted_iota(jnp.int32, (1, GROUP, half * GROUP), 1)
    col = lax.broadcasted_iota(jnp.int32, (1, GROUP, half * GROUP), 2) % GROUP
    keep_wide = own == col

    def forward_part(h, low, high):
        def one(g, carry):
            left = [
                kt_ref[g, k, h * half : (h + 1) * half].reshape(half * GROUP, sources)
                for k in range(2)
            ]
            out = dot(left[0], x_ref[g, 0], NT) + dot(left[1], x_ref[g, 1], NT)
            kept = jnp.where(keep, out.reshape(half, GROUP, columns), 0.0).astype(jnp.bfloat16)
            block = dot(pick_ref[...], kept.reshape(half * GROUP, columns))
            et_ref[:, :, g] = (
                block.T.astype(jnp.bfloat16).reshape(nprobe, 2, GROUP, half)
            )
            return carry

        lax.fori_loop(low, high, one, 0)

    sends = []

    def predict(h):
        for p in range(nprobe):
            spec = et_ref[p].reshape(2 * freqs, half)
            pred_ref[h, p // nown, p % nown] = dot(spec, inv_ref[...], TN).astype(jnp.bfloat16)
        copies = []
        for d in range(1, n_col):
            copy = send(
                pred_ref.at[h, col_peer(d)],
                pred_in.at[h, d - 1],
                ps_sem.at[h, d - 1],
                pr_sem.at[h, d - 1],
                (me_row, col_peer(d)),
            )
            copy.start()
            copies.append(copy)
        sends.extend(copies)
        return copies

    def weigh(h, copies):
        total = pred_ref[h, me_col].astype(jnp.float32)
        for d in range(1, n_col):
            copies[d - 1].wait_recv()
            total = total + pred_in[h, d - 1].astype(jnp.float32)
        scale = weight_ref[h * half : (h + 1) * half, :]
        wt_ref[h, me_col] = (total * scale[None]).astype(jnp.bfloat16)
        out = []
        for d in range(1, n_col):
            copy = send(
                wt_ref.at[h, me_col],
                wt_ref.at[h, me_col],
                ws_sem.at[h, d - 1],
                wr_sem.at[h, d - 1],
                (me_row, col_peer(d)),
            )
            copy.start()
            out.append(copy)
        sends.extend(out)
        return out

    def residual(h, copies):
        for copy in copies:
            copy.wait_recv()
        for p in range(nprobe):
            spec = dot(inv_ref[...], wt_ref[h, p // nown, p % nown], NT).astype(jnp.bfloat16)
            for k in range(2):
                at = (2 * p + k) * GROUP
                y_ref[:, at : at + GROUP, :] = spec[k * freqs : (k + 1) * freqs].reshape(
                    groups, GROUP, half
                )

    def adjoint_part(h, low, high):
        def one(g, carry):
            wide = dot(y_ref[g], pick_ref[...]).reshape(2 * nprobe, GROUP, half * GROUP)
            wide = jnp.where(keep_wide, wide, 0.0).astype(jnp.bfloat16)
            wide = wide.reshape(columns, half * GROUP)
            both = [
                dot(
                    wide, kt_ref[g, k, h * half : (h + 1) * half].reshape(half * GROUP, sources)
                ).reshape(nprobe, 2, GROUP, sources)
                for k in range(2)
            ]
            real = both[0][:, 0] + both[1][:, 1]
            imag = both[0][:, 1] - both[1][:, 0]
            if h > 0:
                real = real + acc_ref[g, 0]
                imag = imag + acc_ref[g, 1]
            if h < halves - 1:
                acc_ref[g, 0] = real
                acc_ref[g, 1] = imag
            else:
                g_ref[:, 0, g] = real.astype(jnp.bfloat16)
                g_ref[:, 1, g] = imag.astype(jnp.bfloat16)
            return carry

        lax.fori_loop(low, high, one, 0)

    mid = groups // 2
    forward_part(0, 0, groups)
    pred_copies = predict(0)
    for h in range(1, halves):
        forward_part(h, 0, mid)
        wt_copies = weigh(h - 1, pred_copies)
        forward_part(h, mid, groups)
        pred_copies = predict(h)
        residual(h - 1, wt_copies)
        adjoint_part(h - 1, 0, mid)
        wt_copies = weigh(h, pred_copies)
        adjoint_part(h - 1, mid, groups)
    if halves == 1:
        wt_copies = weigh(0, pred_copies)
    residual(halves - 1, wt_copies)
    adjoint_part(halves - 1, 0, groups)

    def history(p):
        return dot(g_ref[p].reshape(2 * freqs, sources), fwd_t_ref[...], TN).astype(jnp.bfloat16)

    backs = []
    for d in range(1, n_row):
        peer = row_peer(d)
        for j in range(nloc):
            hess_out[d - 1, j] = history(peer * nloc + j)
        copy = send(
            hess_out.at[d - 1],
            hess_in.at[d - 1],
            hs_sem.at[d - 1],
            hr_sem.at[d - 1],
            (peer, me_col),
        )
        copy.start()
        backs.append(copy)
    for j in range(nloc):
        total = history(me_row * nloc + j).astype(jnp.float32)
        out_ref[j] = total
    for d in range(1, n_row):
        backs[d - 1].wait_recv()
        for j in range(nloc):
            out_ref[j] += hess_in[d - 1, j].astype(jnp.float32)
    for copy in gathers + sends + backs:
        copy.wait_send()


def fused_call(mesh_sizes, kernel_spectra, probes, weight, fwd_t, inverse):
    n_row, n_col = mesh_sizes
    _, sensors, sources, freqs = kernel_spectra.shape
    nloc, _, times = probes.shape
    nprobe = nloc * n_row
    nown = nprobe // n_col
    groups = freqs // GROUP
    columns = nprobe * 2 * GROUP
    halves = HALVES
    half = sensors // halves
    rows = 16
    owner = np.arange(half * GROUP)[None, :] // GROUP
    pick = jnp.asarray((np.arange(half)[:, None] == owner).astype(ml_dtypes.bfloat16))
    vmem = pl.BlockSpec(memory_space=pltpu.VMEM)
    low = jnp.bfloat16
    dma = pltpu.SemaphoreType.DMA
    return pl.pallas_call(
        functools.partial(fused_kernel, n_row, n_col, halves),
        in_specs=[pl.BlockSpec(memory_space=pl.ANY)] + [vmem] * 5,
        out_specs=vmem,
        out_shape=jax.ShapeDtypeStruct(probes.shape, jnp.float32),
        scratch_shapes=[
            pltpu.VMEM((2, 2, rows, sources, freqs), low),
            pltpu.VMEM((groups, 2, sensors, GROUP, sources), low),
            pltpu.VMEM((n_row,) + probes.shape, low),
            pltpu.VMEM((groups, 2, columns, sources), low),
            pltpu.VMEM((nprobe, 2, groups, GROUP, half), low),
            pltpu.VMEM((halves, n_col, nown, half, times), low),
            pltpu.VMEM((halves, n_col - 1, nown, half, times), low),
            pltpu.VMEM((halves, n_col, nown, half, times), low),
            pltpu.VMEM((groups, columns, half), low),
            pltpu.VMEM((groups, 2, nprobe, GROUP, sources), jnp.float32),
            pltpu.VMEM((nprobe, 2, groups, GROUP, sources), low),
            pltpu.VMEM((n_row - 1,) + probes.shape, low),
            pltpu.VMEM((n_row - 1,) + probes.shape, low),
            dma((2,)),
            dma((n_row,)),
            dma((n_row,)),
            dma((halves, n_col - 1)),
            dma((halves, n_col - 1)),
            dma((halves, n_col - 1)),
            dma((halves, n_col - 1)),
            dma((n_row - 1,)),
            dma((n_row - 1,)),
        ],
        compiler_params=pltpu.CompilerParams(
            vmem_limit_bytes=60 * 1024 * 1024, collective_id=0, has_side_effects=True
        ),
        name="fused",
    )(kernel_spectra, probes, weight, fwd_t, inverse, pick)


def plain_forward(kernel_spectra, probes, fwd_t, inv_t):
    freqs = kernel_spectra.shape[3]
    spec = jnp.einsum("Ft,pst->psF", fwd_t, probes, preferred_element_type=jnp.float32)
    spec = spec.astype(jnp.bfloat16)
    spec = spec.reshape(spec.shape[:2] + (2, freqs))
    a = jnp.einsum("krsf,psjf->kjprf", kernel_spectra, spec, preferred_element_type=jnp.float32)
    both = jnp.concatenate([a[0, 0] - a[1, 1], a[0, 1] + a[1, 0]], axis=-1).astype(jnp.bfloat16)
    pred = jnp.einsum("tF,prF->ptr", inv_t, both, preferred_element_type=jnp.float32)
    return kernel_spectra, pred.astype(jnp.bfloat16)


def plain_adjoint(kernel_spectra, weighted, inverse, synthesis):
    freqs = kernel_spectra.shape[3]
    spec = jnp.einsum("Ft,ptr->prF", inverse, weighted, preferred_element_type=jnp.float32)
    spec = spec.astype(jnp.bfloat16)
    spec = spec.reshape(spec.shape[:2] + (2, freqs))
    a = jnp.einsum("krsf,prjf->kjpsf", kernel_spectra, spec, preferred_element_type=jnp.float32)
    both = jnp.concatenate([a[0, 0] + a[1, 1], a[0, 1] - a[1, 0]], axis=-1).astype(jnp.bfloat16)
    out = jnp.einsum("psF,Ft->pst", both, synthesis, preferred_element_type=jnp.float32)
    return out.astype(jnp.bfloat16)


def plain(kernel_spectra, probes, record_weight, fwd_t, inverse):
    gathered = lax.all_gather(probes, "row", axis=0, tiled=True)
    turned, pred = plain_forward(kernel_spectra, gathered, fwd_t, inverse.T)
    predicted = lax.psum_scatter(pred, "col", scatter_dimension=0, tiled=True)
    weighted = (predicted.astype(jnp.float32) * record_weight[None, None, :]).astype(jnp.bfloat16)
    weighted = lax.all_gather(weighted, "col", axis=0, tiled=True)
    part = plain_adjoint(turned, weighted, inverse, fwd_t)
    return lax.psum_scatter(part, "row", scatter_dimension=0, tiled=True).astype(jnp.float32)


def body(sizes, probes, kernel_spectra, sensor_mask, precision, source_block, damping):
    forward, inverse = dft_tables(probes.shape[2])
    fwd_t, inverse = jnp.asarray(forward.T), jnp.asarray(inverse)
    _, sensors, sources, freqs = kernel_spectra.shape
    record_weight = jnp.where(sensor_mask == 1, precision, jnp.zeros_like(precision))
    if sensors % 128 == 0 and sources % 128 == 0 and freqs % 128 == 0:
        summed = fused_call(sizes, kernel_spectra, probes, record_weight[:, None], fwd_t, inverse)
    else:
        summed = plain(kernel_spectra, probes, record_weight, fwd_t, inverse)
    groups = jnp.arange(damping.shape[0], dtype=jnp.int32)
    one_hot = (source_block[:, None] == groups[None, :]).astype(jnp.float32)
    source_damping = jnp.dot(one_hot, damping, precision=lax.Precision.HIGHEST)
    return summed + source_damping[None, :, None] * probes.astype(jnp.float32)


def solution(mesh):
    placed = (P("row", "col", None), P(None, "row", "col", None), P("row"), P("row"), P("col"), P())
    sizes = (mesh.shape["row"], mesh.shape["col"])
    return jax.shard_map(
        functools.partial(body, sizes),
        mesh=mesh,
        in_specs=placed,
        out_specs=P("row", "col", None),
        check_vma=False,
    )
```

```python
import functools
import math

import jax
import jax.numpy as jnp
import ml_dtypes
import numpy as np
from jax import lax
from jax.experimental import pallas as pl
from jax.experimental.pallas import tpu as pltpu
from jax.sharding import PartitionSpec as P

GROUP = 16
HALVES = 2
DEPTH = 8
LANES = 128
MESH = pl.DeviceIdType.MESH
NT = (((1,), (1,)), ((), ()))
TN = (((0,), (0,)), ((), ()))


def dft_tables(length):
    period = 2 * length
    positions = np.arange(length)
    phases = positions[:, None] * positions[None, :] % period
    angles = phases * (2.0 * math.pi / period)
    cosine = np.cos(angles).astype(np.float32)
    sines = np.sin(angles).astype(np.float32)
    weight = (np.where(positions == 0, 1.0, 2.0) / period).astype(np.float32)
    forward = np.concatenate([cosine, -sines], axis=1).astype(ml_dtypes.bfloat16)
    inverse = np.concatenate([cosine * weight[:, None], -sines * weight[:, None]], axis=0).astype(
        ml_dtypes.bfloat16
    )
    return (forward, inverse)


def dot(a, b, dims=None):
    if dims is None:
        return jnp.dot(a, b, preferred_element_type=jnp.float32)
    return lax.dot_general(a, b, dims, preferred_element_type=jnp.float32)


def fused_kernel(
    n_row,
    n_col,
    halves,
    k_hbm,
    probes_ref,
    mask_ref,
    precision_ref,
    block_ref,
    damping_ref,
    fwd_t_ref,
    inv_ref,
    pick_ref,
    out_ref,
    stage,
    kt_first,
    kt_last,
    gath,
    x_ref,
    et_ref,
    pred_ref,
    pred_in,
    wt_ref,
    y_ref,
    acc_ref,
    g_ref,
    hess_out,
    hess_in,
    k_sem,
    gs_sem,
    gr_sem,
    ps_sem,
    pr_sem,
    ws_sem,
    wr_sem,
    hs_sem,
    hr_sem,
):
    me_row, me_col = lax.axis_index("row"), lax.axis_index("col")
    _, sensors, sources, freqs = k_hbm.shape
    nloc = probes_ref.shape[0]
    nprobe = nloc * n_row
    nown = nprobe // n_col
    groups = freqs // GROUP
    columns = nprobe * 2 * GROUP
    depth, _, rows, _, _ = stage.shape
    steps = sensors // rows
    half = sensors // halves
    kts = [kt_first, kt_last]

    def row_peer(d):
        return lax.rem(me_row + d, n_row)

    def col_peer(d):
        return lax.rem(me_col + d, n_col)

    def load(step, slot):
        at = pl.ds(pl.multiple_of(step * rows, rows), rows)
        return pltpu.make_async_copy(k_hbm.at[:, at], stage.at[slot], k_sem.at[slot])

    for slot in range(depth):
        load(slot, slot).start()

    barrier = pltpu.get_barrier_semaphore()
    for d in range(1, n_row):
        pl.semaphore_signal(barrier, inc=1, device_id=(row_peer(d), me_col), device_id_type=MESH)
    for d in range(1, n_col):
        pl.semaphore_signal(barrier, inc=1, device_id=(me_row, col_peer(d)), device_id_type=MESH)
    pl.semaphore_wait(barrier, n_row + n_col - 2)

    def send(src, dst, send_sem, recv_sem, device):
        return pltpu.make_async_remote_copy(
            src_ref=src,
            dst_ref=dst,
            send_sem=send_sem,
            recv_sem=recv_sem,
            device_id=device,
            device_id_type=MESH,
        )

    gathers = []
    for d in range(1, n_row):
        copy = send(
            probes_ref,
            gath.at[d],
            gs_sem.at[d],
            gr_sem.at[d],
            (row_peer(d), me_col),
        )
        copy.start()
        gathers.append(copy)

    def turn(kt, slot, r, row):
        for k in range(2):
            kt[:, k, row, :, :] = stage[slot, k, r].T.reshape(groups, GROUP, sources)

    def load_next(step, slot):
        @pl.when(step + depth < steps)
        def _():
            load(step + depth, slot).start()

    def turn_first(step, carry):
        slot = lax.rem(step, depth)
        load(step, slot).wait()
        for r in range(rows):
            turn(kt_first, slot, r, step * rows + r)
        load_next(step, slot)
        return carry

    lax.fori_loop(0, groups, turn_first, 0)

    def spectra(p, block):
        spec = dot(fwd_t_ref[...], block, NT).astype(jnp.bfloat16)
        real = spec[:freqs].reshape(groups, GROUP, sources)
        imag = spec[freqs:].reshape(groups, GROUP, sources)
        first = pl.ds(pl.multiple_of(p * 2 * GROUP, GROUP), GROUP)
        second = pl.ds(pl.multiple_of(p * 2 * GROUP + GROUP, GROUP), GROUP)
        x_ref[:, 0, first, :] = real
        x_ref[:, 0, second, :] = imag
        x_ref[:, 1, first, :] = -imag
        x_ref[:, 1, second, :] = real

    for j in range(nloc):
        spectra(me_row * nloc + j, probes_ref[j])
    for d in range(1, n_row):
        gathers[d - 1].wait_recv()
        origin = lax.rem(me_row + n_row - d, n_row)
        for j in range(nloc):
            spectra(origin * nloc + j, gath[d, j])

    def column(row, width):
        tall = jnp.broadcast_to(row, (LANES, row.shape[1])).T
        return jnp.concatenate([tall] * (width // LANES), axis=1)

    times = probes_ref.shape[2]
    precision = precision_ref[...]
    sensor_weight = column(
        jnp.where(mask_ref[...] == 1, precision, jnp.zeros_like(precision)), times
    )

    own = lax.broadcasted_iota(jnp.int32, (1, GROUP, columns), 1)
    col = lax.broadcasted_iota(jnp.int32, (1, GROUP, columns), 2) % GROUP
    keep = own == col
    own = lax.broadcasted_iota(jnp.int32, (1, GROUP, half * GROUP), 1)
    col = lax.broadcasted_iota(jnp.int32, (1, GROUP, half * GROUP), 2) % GROUP
    keep_wide = own == col

    def forward_chunk(h, g, first, count):
        left = [
            kts[h][g, k, first : first + count].reshape(count * GROUP, sources) for k in range(2)
        ]
        out = dot(left[0], x_ref[g, 0], NT) + dot(left[1], x_ref[g, 1], NT)
        kept = jnp.where(keep, out.reshape(count, GROUP, columns), 0.0).astype(jnp.bfloat16)
        return dot(pick_ref[:count, : count * GROUP], kept.reshape(count * GROUP, columns))

    def store_blocks(g, block):
        et_ref[:, :, g] = block.T.astype(jnp.bfloat16).reshape(nprobe, 2, GROUP, half)

    def forward_turning(g, carry):
        step = groups + g
        slot = lax.rem(step, depth)
        load(step, slot).wait()
        count = half // 2
        blocks = []
        for piece in range(2):
            for r in range(piece * rows // 2, (piece + 1) * rows // 2):
                turn(kt_last, slot, r, g * rows + r)
            blocks.append(forward_chunk(0, g, piece * count, count))
        store_blocks(g, jnp.concatenate(blocks, axis=0))
        load_next(step, slot)
        return carry

    def forward_part(h, low, high):
        def one(g, carry):
            store_blocks(g, forward_chunk(h, g, 0, half))
            return carry

        lax.fori_loop(low, high, one, 0, unroll=2)

    sends = []

    def predict(h):
        for p in range(nprobe):
            spec = et_ref[p].reshape(2 * freqs, half)
            pred_ref[h, p // nown, p % nown] = dot(spec, inv_ref[...], TN).astype(jnp.bfloat16)
        copies = []
        for d in range(1, n_col):
            copy = send(
                pred_ref.at[h, col_peer(d)],
                pred_in.at[h, d - 1],
                ps_sem.at[h, d - 1],
                pr_sem.at[h, d - 1],
                (me_row, col_peer(d)),
            )
            copy.start()
            copies.append(copy)
        sends.extend(copies)
        return copies

    def weigh(h, copies):
        total = pred_ref[h, me_col].astype(jnp.float32)
        for d in range(1, n_col):
            copies[d - 1].wait_recv()
            total = total + pred_in[h, d - 1].astype(jnp.float32)
        scale = sensor_weight[h * half : (h + 1) * half]
        wt_ref[h, me_col] = (total * scale[None]).astype(jnp.bfloat16)
        out = []
        for d in range(1, n_col):
            copy = send(
                wt_ref.at[h, me_col],
                wt_ref.at[h, me_col],
                ws_sem.at[h, d - 1],
                wr_sem.at[h, d - 1],
                (me_row, col_peer(d)),
            )
            copy.start()
            out.append(copy)
        sends.extend(out)
        return out

    def residual(h, copies):
        for copy in copies:
            copy.wait_recv()
        for p in range(nprobe):
            spec = dot(inv_ref[...], wt_ref[h, p // nown, p % nown], NT).astype(jnp.bfloat16)
            for k in range(2):
                at = (2 * p + k) * GROUP
                y_ref[:, at : at + GROUP, :] = spec[k * freqs : (k + 1) * freqs].reshape(
                    groups, GROUP, half
                )

    def adjoint_part(h, low, high):
        def one(g, carry):
            wide = dot(y_ref[g], pick_ref[...]).reshape(2 * nprobe, GROUP, half * GROUP)
            wide = jnp.where(keep_wide, wide, 0.0).astype(jnp.bfloat16)
            wide = wide.reshape(columns, half * GROUP)
            both = [
                dot(
                    wide, kts[h][g, k].reshape(half * GROUP, sources)
                ).reshape(nprobe, 2, GROUP, sources)
                for k in range(2)
            ]
            real = both[0][:, 0] + both[1][:, 1]
            imag = both[0][:, 1] - both[1][:, 0]
            if h > 0:
                real = real + acc_ref[g, 0]
                imag = imag + acc_ref[g, 1]
            if h < halves - 1:
                acc_ref[g, 0] = real
                acc_ref[g, 1] = imag
            else:
                g_ref[:, 0, g] = real.astype(jnp.bfloat16)
                g_ref[:, 1, g] = imag.astype(jnp.bfloat16)
            return carry

        lax.fori_loop(low, high, one, 0, unroll=2)

    mid = groups // 2
    lax.fori_loop(0, groups, forward_turning, 0)
    pred_copies = predict(0)
    for h in range(1, halves):
        forward_part(h, 0, mid)
        wt_copies = weigh(h - 1, pred_copies)
        forward_part(h, mid, groups)
        pred_copies = predict(h)
        residual(h - 1, wt_copies)
        adjoint_part(h - 1, 0, mid)
        wt_copies = weigh(h, pred_copies)
        adjoint_part(h - 1, mid, groups)
    residual(halves - 1, wt_copies)
    adjoint_part(halves - 1, 0, groups)

    def history(p):
        return dot(g_ref[p].reshape(2 * freqs, sources), fwd_t_ref[...], TN).astype(jnp.bfloat16)

    backs = []
    for d in range(1, n_row):
        peer = row_peer(d)
        for j in range(nloc):
            hess_out[d - 1, j] = history(peer * nloc + j)
        copy = send(
            hess_out.at[d - 1],
            hess_in.at[d - 1],
            hs_sem.at[d - 1],
            hr_sem.at[d - 1],
            (peer, me_col),
        )
        copy.start()
        backs.append(copy)
    group_of = block_ref[...]
    damp = jnp.zeros(group_of.shape, jnp.float32)
    for n in range(damping_ref.shape[0]):
        damp = jnp.where(group_of == n, damping_ref[n], damp)
    damp = column(damp, times)
    for j in range(nloc):
        total = history(me_row * nloc + j).astype(jnp.float32)
        out_ref[j] = total + damp * probes_ref[j].astype(jnp.float32)
    for d in range(1, n_row):
        backs[d - 1].wait_recv()
        for j in range(nloc):
            out_ref[j] += hess_in[d - 1, j].astype(jnp.float32)
    for copy in gathers + sends + backs:
        copy.wait_send()


def fused_call(
    mesh_sizes,
    kernel_spectra,
    probes,
    sensor_mask,
    precision,
    source_block,
    damping,
    fwd_t,
    inverse,
):
    n_row, n_col = mesh_sizes
    _, sensors, sources, freqs = kernel_spectra.shape
    nloc, _, times = probes.shape
    nprobe = nloc * n_row
    nown = nprobe // n_col
    groups = freqs // GROUP
    columns = nprobe * 2 * GROUP
    halves = HALVES
    half = sensors // halves
    rows = half // groups
    owner = np.arange(half * GROUP)[None, :] // GROUP
    pick = jnp.asarray((np.arange(half)[:, None] == owner).astype(ml_dtypes.bfloat16))
    vmem = pl.BlockSpec(memory_space=pltpu.VMEM)
    low = jnp.bfloat16
    dma = pltpu.SemaphoreType.DMA
    return pl.pallas_call(
        functools.partial(fused_kernel, n_row, n_col, halves),
        in_specs=[pl.BlockSpec(memory_space=pl.ANY)]
        + [vmem] * 4
        + [pl.BlockSpec(memory_space=pltpu.SMEM)]
        + [vmem] * 3,
        out_specs=vmem,
        out_shape=jax.ShapeDtypeStruct(probes.shape, jnp.float32),
        scratch_shapes=[
            pltpu.VMEM((DEPTH, 2, rows, sources, freqs), low),
            pltpu.VMEM((groups, 2, half, GROUP, sources), low),
            pltpu.VMEM((groups, 2, half, GROUP, sources), low),
            pltpu.VMEM((n_row,) + probes.shape, low),
            pltpu.VMEM((groups, 2, columns, sources), low),
            pltpu.VMEM((nprobe, 2, groups, GROUP, half), low),
            pltpu.VMEM((halves, n_col, nown, half, times), low),
            pltpu.VMEM((halves, n_col - 1, nown, half, times), low),
            pltpu.VMEM((halves, n_col, nown, half, times), low),
            pltpu.VMEM((groups, columns, half), low),
            pltpu.VMEM((groups, 2, nprobe, GROUP, sources), jnp.float32),
            pltpu.VMEM((nprobe, 2, groups, GROUP, sources), low),
            pltpu.VMEM((n_row - 1,) + probes.shape, low),
            pltpu.VMEM((n_row - 1,) + probes.shape, low),
            dma((DEPTH,)),
            dma((n_row,)),
            dma((n_row,)),
            dma((halves, n_col - 1)),
            dma((halves, n_col - 1)),
            dma((halves, n_col - 1)),
            dma((halves, n_col - 1)),
            dma((n_row - 1,)),
            dma((n_row - 1,)),
        ],
        compiler_params=pltpu.CompilerParams(
            vmem_limit_bytes=60 * 1024 * 1024, collective_id=0, has_side_effects=True
        ),
        name="fused",
    )(
        kernel_spectra,
        probes,
        sensor_mask[None, :],
        precision[None, :],
        source_block[None, :],
        damping,
        fwd_t,
        inverse,
        pick,
    )


def plain_forward(kernel_spectra, probes, fwd_t, inv_t):
    freqs = kernel_spectra.shape[3]
    spec = jnp.einsum("Ft,pst->psF", fwd_t, probes, preferred_element_type=jnp.float32)
    spec = spec.astype(jnp.bfloat16)
    spec = spec.reshape(spec.shape[:2] + (2, freqs))
    a = jnp.einsum("krsf,psjf->kjprf", kernel_spectra, spec, preferred_element_type=jnp.float32)
    both = jnp.concatenate([a[0, 0] - a[1, 1], a[0, 1] + a[1, 0]], axis=-1).astype(jnp.bfloat16)
    pred = jnp.einsum("tF,prF->ptr", inv_t, both, preferred_element_type=jnp.float32)
    return kernel_spectra, pred.astype(jnp.bfloat16)


def plain_adjoint(kernel_spectra, weighted, inverse, synthesis):
    freqs = kernel_spectra.shape[3]
    spec = jnp.einsum("Ft,ptr->prF", inverse, weighted, preferred_element_type=jnp.float32)
    spec = spec.astype(jnp.bfloat16)
    spec = spec.reshape(spec.shape[:2] + (2, freqs))
    a = jnp.einsum("krsf,prjf->kjpsf", kernel_spectra, spec, preferred_element_type=jnp.float32)
    both = jnp.concatenate([a[0, 0] + a[1, 1], a[0, 1] - a[1, 0]], axis=-1).astype(jnp.bfloat16)
    out = jnp.einsum("psF,Ft->pst", both, synthesis, preferred_element_type=jnp.float32)
    return out.astype(jnp.bfloat16)


def plain(kernel_spectra, probes, record_weight, fwd_t, inverse):
    gathered = lax.all_gather(probes, "row", axis=0, tiled=True)
    turned, pred = plain_forward(kernel_spectra, gathered, fwd_t, inverse.T)
    predicted = lax.psum_scatter(pred, "col", scatter_dimension=0, tiled=True)
    weighted = (predicted.astype(jnp.float32) * record_weight[None, None, :]).astype(jnp.bfloat16)
    weighted = lax.all_gather(weighted, "col", axis=0, tiled=True)
    part = plain_adjoint(turned, weighted, inverse, fwd_t)
    return lax.psum_scatter(part, "row", scatter_dimension=0, tiled=True).astype(jnp.float32)


def body(sizes, probes, kernel_spectra, sensor_mask, precision, source_block, damping):
    forward, inverse = dft_tables(probes.shape[2])
    fwd_t, inverse = jnp.asarray(forward.T), jnp.asarray(inverse)
    _, sensors, sources, freqs = kernel_spectra.shape
    half, groups = sensors // HALVES, freqs // GROUP
    aligned = all(size % LANES == 0 for size in (sensors, sources, freqs))
    if aligned and half % (2 * groups) == 0 and sensors // (half // groups) >= DEPTH:
        return fused_call(
            sizes,
            kernel_spectra,
            probes,
            sensor_mask,
            precision,
            source_block,
            damping,
            fwd_t,
            inverse,
        )
    record_weight = jnp.where(sensor_mask == 1, precision, jnp.zeros_like(precision))
    summed = plain(kernel_spectra, probes, record_weight, fwd_t, inverse)
    numbers = jnp.arange(damping.shape[0], dtype=jnp.int32)
    one_hot = (source_block[:, None] == numbers[None, :]).astype(jnp.float32)
    source_damping = jnp.dot(one_hot, damping, precision=lax.Precision.HIGHEST)
    return summed + source_damping[None, :, None] * probes.astype(jnp.float32)


def solution(mesh):
    placed = (P("row", "col", None), P(None, "row", "col", None), P("row"), P("row"), P("col"), P())
    sizes = (mesh.shape["row"], mesh.shape["col"])
    return jax.shard_map(
        functools.partial(body, sizes),
        mesh=mesh,
        in_specs=placed,
        out_specs=P("row", "col", None),
        check_vma=False,
    )
```

```python
import functools
import math

import jax
import jax.numpy as jnp
import ml_dtypes
import numpy as np
from jax import lax
from jax.experimental import pallas as pl
from jax.experimental.pallas import tpu as pltpu
from jax.sharding import PartitionSpec as P

GROUP = 16
HALVES = 2
DEPTH = 8
LANES = 128
MESH = pl.DeviceIdType.MESH
NT = (((1,), (1,)), ((), ()))
TN = (((0,), (0,)), ((), ()))


def dft_tables(length):
    period = 2 * length
    positions = np.arange(length)
    phases = positions[:, None] * positions[None, :] % period
    angles = phases * (2.0 * math.pi / period)
    cosine = np.cos(angles).astype(np.float32)
    sines = np.sin(angles).astype(np.float32)
    weight = (np.where(positions == 0, 1.0, 2.0) / period).astype(np.float32)
    forward = np.concatenate([cosine, -sines], axis=1).astype(ml_dtypes.bfloat16)
    inverse = np.concatenate([cosine * weight[:, None], -sines * weight[:, None]], axis=0).astype(
        ml_dtypes.bfloat16
    )
    return (forward, inverse)


def dot(a, b, dims=None):
    if dims is None:
        return jnp.dot(a, b, preferred_element_type=jnp.float32)
    return lax.dot_general(a, b, dims, preferred_element_type=jnp.float32)


def fused_kernel(
    n_row,
    n_col,
    halves,
    k_hbm,
    probes_ref,
    mask_ref,
    precision_ref,
    block_ref,
    damping_ref,
    fwd_t_ref,
    inv_ref,
    pick_ref,
    out_ref,
    stage,
    kt_first,
    kt_last,
    gath,
    x_ref,
    et_ref,
    pred_ref,
    pred_in,
    wt_ref,
    y_ref,
    acc_ref,
    g_ref,
    wide_even,
    wide_odd,
    pair_out,
    pair_in,
    far_out,
    far_in,
    k_sem,
    gs_sem,
    gr_sem,
    ps_sem,
    pr_sem,
    ws_sem,
    wr_sem,
    hs_sem,
    hr_sem,
    fs_sem,
    fr_sem,
):
    me_row, me_col = lax.axis_index("row"), lax.axis_index("col")
    _, sensors, sources, freqs = k_hbm.shape
    nloc = probes_ref.shape[0]
    nprobe = nloc * n_row
    nown = nprobe // n_col
    groups = freqs // GROUP
    columns = nprobe * 2 * GROUP
    depth, _, rows, _, _ = stage.shape
    steps = sensors // rows
    half = sensors // halves
    kts = [kt_first, kt_last]

    def row_peer(d):
        return lax.rem(me_row + d, n_row)

    def col_peer(d):
        return lax.rem(me_col + d, n_col)

    def load(step, slot):
        at = pl.ds(pl.multiple_of(step * rows, rows), rows)
        return pltpu.make_async_copy(k_hbm.at[:, at], stage.at[slot], k_sem.at[slot])

    for slot in range(depth):
        load(slot, slot).start()

    barrier = pltpu.get_barrier_semaphore()
    for d in range(1, n_row):
        pl.semaphore_signal(barrier, inc=1, device_id=(row_peer(d), me_col), device_id_type=MESH)
    for d in range(1, n_col):
        pl.semaphore_signal(barrier, inc=1, device_id=(me_row, col_peer(d)), device_id_type=MESH)
    pl.semaphore_wait(barrier, n_row + n_col - 2)

    def send(src, dst, send_sem, recv_sem, device):
        return pltpu.make_async_remote_copy(
            src_ref=src,
            dst_ref=dst,
            send_sem=send_sem,
            recv_sem=recv_sem,
            device_id=device,
            device_id_type=MESH,
        )

    gathers = []
    for d in range(1, n_row):
        copy = send(
            probes_ref,
            gath.at[d],
            gs_sem.at[d],
            gr_sem.at[d],
            (row_peer(d), me_col),
        )
        copy.start()
        gathers.append(copy)

    def turn(kt, slot, r, row):
        for k in range(2):
            kt[:, k, row, :, :] = stage[slot, k, r].T.reshape(groups, GROUP, sources)

    def load_next(step, slot):
        @pl.when(step + depth < steps)
        def _():
            load(step + depth, slot).start()

    def turn_first(step, carry):
        slot = lax.rem(step, depth)
        load(step, slot).wait()
        for r in range(rows):
            turn(kt_first, slot, r, step * rows + r)
        load_next(step, slot)
        return carry

    lax.fori_loop(0, groups, turn_first, 0)

    def spectra(p, block):
        spec = dot(fwd_t_ref[...], block, NT).astype(jnp.bfloat16)
        real = spec[:freqs].reshape(groups, GROUP, sources)
        imag = spec[freqs:].reshape(groups, GROUP, sources)
        first = pl.ds(pl.multiple_of(p * 2 * GROUP, GROUP), GROUP)
        second = pl.ds(pl.multiple_of(p * 2 * GROUP + GROUP, GROUP), GROUP)
        x_ref[:, first, :sources] = real
        x_ref[:, second, :sources] = imag
        x_ref[:, first, sources:] = -imag
        x_ref[:, second, sources:] = real

    for j in range(nloc):
        spectra(me_row * nloc + j, probes_ref[j])
    for d in range(1, n_row):
        gathers[d - 1].wait_recv()
        origin = lax.rem(me_row + n_row - d, n_row)
        for j in range(nloc):
            spectra(origin * nloc + j, gath[d, j])

    def column(row, width):
        tall = jnp.broadcast_to(row, (LANES, row.shape[1])).T
        return jnp.concatenate([tall] * (width // LANES), axis=1)

    times = probes_ref.shape[2]
    precision = precision_ref[...]
    sensor_weight = column(
        jnp.where(mask_ref[...] == 1, precision, jnp.zeros_like(precision)), times
    )

    own = lax.broadcasted_iota(jnp.int32, (1, GROUP, columns), 1)
    col = lax.broadcasted_iota(jnp.int32, (1, GROUP, columns), 2) % GROUP
    keep = own == col
    own = lax.broadcasted_iota(jnp.int32, (1, GROUP, half * GROUP), 1)
    col = lax.broadcasted_iota(jnp.int32, (1, GROUP, half * GROUP), 2) % GROUP
    keep_wide = own == col

    def forward_chunk(h, g, first, count):
        left = [
            kts[h][g, k, first : first + count].reshape(count * GROUP, sources) for k in range(2)
        ]
        out = dot(jnp.concatenate(left, axis=1), x_ref[g], NT)
        kept = jnp.where(keep, out.reshape(count, GROUP, columns), 0.0).astype(jnp.bfloat16)
        return dot(pick_ref[:count, : count * GROUP], kept.reshape(count * GROUP, columns))

    def store_blocks(g, block):
        et_ref[:, :, g] = block.T.astype(jnp.bfloat16).reshape(nprobe, 2, GROUP, half)

    def forward_turning(g, carry):
        step = groups + g
        slot = lax.rem(step, depth)
        load(step, slot).wait()
        count = half // 2
        blocks = []
        for piece in range(2):
            for r in range(piece * rows // 2, (piece + 1) * rows // 2):
                turn(kt_last, slot, r, g * rows + r)
            blocks.append(forward_chunk(0, g, piece * count, count))
        store_blocks(g, jnp.concatenate(blocks, axis=0))
        load_next(step, slot)
        return carry

    def forward_part(h, low, high):
        def one(g, carry):
            store_blocks(g, forward_chunk(h, g, 0, half))
            return carry

        lax.fori_loop(low, high, one, 0, unroll=2)

    sends = []

    def predict(h):
        for p in range(nprobe):
            spec = et_ref[p].reshape(2 * freqs, half)
            pred_ref[h, p // nown, p % nown] = dot(spec, inv_ref[...], TN).astype(jnp.bfloat16)
        copies = []
        for d in range(1, n_col):
            copy = send(
                pred_ref.at[h, col_peer(d)],
                pred_in.at[h, d - 1],
                ps_sem.at[h, d - 1],
                pr_sem.at[h, d - 1],
                (me_row, col_peer(d)),
            )
            copy.start()
            copies.append(copy)
        sends.extend(copies)
        return copies

    def weigh(h, copies):
        total = pred_ref[h, me_col].astype(jnp.float32)
        for d in range(1, n_col):
            copies[d - 1].wait_recv()
            total = total + pred_in[h, d - 1].astype(jnp.float32)
        scale = sensor_weight[h * half : (h + 1) * half]
        wt_ref[h, me_col] = (total * scale[None]).astype(jnp.bfloat16)
        out = []
        for d in range(1, n_col):
            copy = send(
                wt_ref.at[h, me_col],
                wt_ref.at[h, me_col],
                ws_sem.at[h, d - 1],
                wr_sem.at[h, d - 1],
                (me_row, col_peer(d)),
            )
            copy.start()
            out.append(copy)
        sends.extend(out)
        return out

    def residual(h, copies):
        for copy in copies:
            copy.wait_recv()
        for p in range(nprobe):
            spec = dot(inv_ref[...], wt_ref[h, p // nown, p % nown], NT).astype(jnp.bfloat16)
            for k in range(2):
                at = (2 * p + k) * GROUP
                y_ref[:, at : at + GROUP, :] = spec[k * freqs : (k + 1) * freqs].reshape(
                    groups, GROUP, half
                )

    def widen(g, wide_ref):
        wide = dot(y_ref[g], pick_ref[...]).reshape(2 * nprobe, GROUP, half * GROUP)
        wide = jnp.where(keep_wide, wide, 0.0).astype(jnp.bfloat16)
        wide_ref[...] = wide.reshape(columns, half * GROUP)

    def multiply(h, g, wide_ref):
        both = [
            dot(wide_ref[...], kts[h][g, k].reshape(half * GROUP, sources)).reshape(
                nprobe, 2, GROUP, sources
            )
            for k in range(2)
        ]
        real = both[0][:, 0] + both[1][:, 1]
        imag = both[0][:, 1] - both[1][:, 0]
        if h > 0:
            real = real + acc_ref[g, 0]
            imag = imag + acc_ref[g, 1]
        if h < halves - 1:
            acc_ref[g, 0] = real
            acc_ref[g, 1] = imag
        else:
            g_ref[:, 0, g] = real.astype(jnp.bfloat16)
            g_ref[:, 1, g] = imag.astype(jnp.bfloat16)

    def adjoint_part(h, low, high):
        widen(low, wide_even)

        def two(i, carry):
            g = low + 2 * i
            widen(g + 1, wide_odd)
            multiply(h, g, wide_even)
            widen(lax.rem(g + 2, groups), wide_even)
            multiply(h, g + 1, wide_odd)
            return carry

        lax.fori_loop(0, (high - low) // 2, two, 0)

    mid = groups // 2
    lax.fori_loop(0, groups, forward_turning, 0)
    pred_copies = predict(0)
    for h in range(1, halves):
        forward_part(h, 0, mid)
        wt_copies = weigh(h - 1, pred_copies)
        forward_part(h, mid, groups)
        pred_copies = predict(h)
        residual(h - 1, wt_copies)
        adjoint_part(h - 1, 0, mid)
        wt_copies = weigh(h, pred_copies)
        adjoint_part(h - 1, mid, groups)
    residual(halves - 1, wt_copies)
    adjoint_part(halves - 1, 0, groups)

    def history(p):
        return dot(g_ref[p].reshape(2 * freqs, sources), fwd_t_ref[...], TN)

    def flip(change):
        place, bit = 0, 1
        while bit < n_row:
            place = place + lax.rem(lax.div(me_row, bit) + (change // bit) % 2, 2) * bit
            bit *= 2
        return place

    changes = list(range(n_row - 2, -1, -2))
    backs, joins = [], []
    for i, change in enumerate(changes):
        peer = flip(change + 1)
        for j in range(nloc):
            pair_out[i, j] = history(peer * nloc + j).astype(jnp.bfloat16)
        copy = send(
            pair_out.at[i], pair_in.at[i], hs_sem.at[i], hr_sem.at[i], (flip(1), me_col)
        )
        copy.start()
        joins.append(copy)
    for i, change in enumerate(changes):
        peer = flip(change)
        total = [history(peer * nloc + j) for j in range(nloc)]
        joins[i].wait_recv()
        total = [total[j] + pair_in[i, j].astype(jnp.float32) for j in range(nloc)]
        if change > 0:
            for j in range(nloc):
                far_out[i, j] = total[j].astype(jnp.bfloat16)
            copy = send(
                far_out.at[i], far_in.at[i], fs_sem.at[i], fr_sem.at[i], (peer, me_col)
            )
            copy.start()
            backs.append(copy)
    group_of = block_ref[...]
    damp = jnp.zeros(group_of.shape, jnp.float32)
    for n in range(damping_ref.shape[0]):
        damp = jnp.where(group_of == n, damping_ref[n], damp)
    damp = column(damp, times)
    for j in range(nloc):
        out_ref[j] = total[j] + damp * probes_ref[j].astype(jnp.float32)
    for i, copy in enumerate(backs):
        copy.wait_recv()
        for j in range(nloc):
            out_ref[j] += far_in[i, j].astype(jnp.float32)
    for copy in gathers + sends + joins + backs:
        copy.wait_send()


def fused_call(
    mesh_sizes,
    kernel_spectra,
    probes,
    sensor_mask,
    precision,
    source_block,
    damping,
    fwd_t,
    inverse,
):
    n_row, n_col = mesh_sizes
    _, sensors, sources, freqs = kernel_spectra.shape
    nloc, _, times = probes.shape
    nprobe = nloc * n_row
    nown = nprobe // n_col
    groups = freqs // GROUP
    columns = nprobe * 2 * GROUP
    halves = HALVES
    half = sensors // halves
    rows = half // groups
    owner = np.arange(half * GROUP)[None, :] // GROUP
    pick = jnp.asarray((np.arange(half)[:, None] == owner).astype(ml_dtypes.bfloat16))
    vmem = pl.BlockSpec(memory_space=pltpu.VMEM)
    low = jnp.bfloat16
    dma = pltpu.SemaphoreType.DMA
    return pl.pallas_call(
        functools.partial(fused_kernel, n_row, n_col, halves),
        in_specs=[pl.BlockSpec(memory_space=pl.ANY)]
        + [vmem] * 4
        + [pl.BlockSpec(memory_space=pltpu.SMEM)]
        + [vmem] * 3,
        out_specs=vmem,
        out_shape=jax.ShapeDtypeStruct(probes.shape, jnp.float32),
        scratch_shapes=[
            pltpu.VMEM((DEPTH, 2, rows, sources, freqs), low),
            pltpu.VMEM((groups, 2, half, GROUP, sources), low),
            pltpu.VMEM((groups, 2, half, GROUP, sources), low),
            pltpu.VMEM((n_row,) + probes.shape, low),
            pltpu.VMEM((groups, columns, 2 * sources), low),
            pltpu.VMEM((nprobe, 2, groups, GROUP, half), low),
            pltpu.VMEM((halves, n_col, nown, half, times), low),
            pltpu.VMEM((halves, n_col - 1, nown, half, times), low),
            pltpu.VMEM((halves, n_col, nown, half, times), low),
            pltpu.VMEM((groups, columns, half), low),
            pltpu.VMEM((groups, 2, nprobe, GROUP, sources), jnp.float32),
            pltpu.VMEM((nprobe, 2, groups, GROUP, sources), low),
            pltpu.VMEM((columns, half * GROUP), low),
            pltpu.VMEM((columns, half * GROUP), low),
            pltpu.VMEM((n_row // 2,) + probes.shape, low),
            pltpu.VMEM((n_row // 2,) + probes.shape, low),
            pltpu.VMEM((n_row // 2 - 1,) + probes.shape, low),
            pltpu.VMEM((n_row // 2 - 1,) + probes.shape, low),
            dma((DEPTH,)),
            dma((n_row,)),
            dma((n_row,)),
            dma((halves, n_col - 1)),
            dma((halves, n_col - 1)),
            dma((halves, n_col - 1)),
            dma((halves, n_col - 1)),
            dma((n_row // 2,)),
            dma((n_row // 2,)),
            dma((n_row // 2 - 1,)),
            dma((n_row // 2 - 1,)),
        ],
        compiler_params=pltpu.CompilerParams(
            vmem_limit_bytes=60 * 1024 * 1024, collective_id=0, has_side_effects=True
        ),
        name="fused",
    )(
        kernel_spectra,
        probes,
        sensor_mask[None, :],
        precision[None, :],
        source_block[None, :],
        damping,
        fwd_t,
        inverse,
        pick,
    )


def plain_forward(kernel_spectra, probes, fwd_t, inv_t):
    freqs = kernel_spectra.shape[3]
    spec = jnp.einsum("Ft,pst->psF", fwd_t, probes, preferred_element_type=jnp.float32)
    spec = spec.astype(jnp.bfloat16)
    spec = spec.reshape(spec.shape[:2] + (2, freqs))
    a = jnp.einsum("krsf,psjf->kjprf", kernel_spectra, spec, preferred_element_type=jnp.float32)
    both = jnp.concatenate([a[0, 0] - a[1, 1], a[0, 1] + a[1, 0]], axis=-1).astype(jnp.bfloat16)
    pred = jnp.einsum("tF,prF->ptr", inv_t, both, preferred_element_type=jnp.float32)
    return kernel_spectra, pred.astype(jnp.bfloat16)


def plain_adjoint(kernel_spectra, weighted, inverse, synthesis):
    freqs = kernel_spectra.shape[3]
    spec = jnp.einsum("Ft,ptr->prF", inverse, weighted, preferred_element_type=jnp.float32)
    spec = spec.astype(jnp.bfloat16)
    spec = spec.reshape(spec.shape[:2] + (2, freqs))
    a = jnp.einsum("krsf,prjf->kjpsf", kernel_spectra, spec, preferred_element_type=jnp.float32)
    both = jnp.concatenate([a[0, 0] + a[1, 1], a[0, 1] - a[1, 0]], axis=-1).astype(jnp.bfloat16)
    out = jnp.einsum("psF,Ft->pst", both, synthesis, preferred_element_type=jnp.float32)
    return out.astype(jnp.bfloat16)


def plain(kernel_spectra, probes, record_weight, fwd_t, inverse):
    gathered = lax.all_gather(probes, "row", axis=0, tiled=True)
    turned, pred = plain_forward(kernel_spectra, gathered, fwd_t, inverse.T)
    predicted = lax.psum_scatter(pred, "col", scatter_dimension=0, tiled=True)
    weighted = (predicted.astype(jnp.float32) * record_weight[None, None, :]).astype(jnp.bfloat16)
    weighted = lax.all_gather(weighted, "col", axis=0, tiled=True)
    part = plain_adjoint(turned, weighted, inverse, fwd_t)
    return lax.psum_scatter(part, "row", scatter_dimension=0, tiled=True).astype(jnp.float32)


def body(sizes, probes, kernel_spectra, sensor_mask, precision, source_block, damping):
    forward, inverse = dft_tables(probes.shape[2])
    fwd_t, inverse = jnp.asarray(forward.T), jnp.asarray(inverse)
    _, sensors, sources, freqs = kernel_spectra.shape
    half, groups = sensors // HALVES, freqs // GROUP
    aligned = all(size % LANES == 0 for size in (sensors, sources, freqs))
    paired = sizes[0] >= 4 and sizes[0] & (sizes[0] - 1) == 0
    if aligned and paired and half % (2 * groups) == 0 and sensors // (half // groups) >= DEPTH:
        return fused_call(
            sizes,
            kernel_spectra,
            probes,
            sensor_mask,
            precision,
            source_block,
            damping,
            fwd_t,
            inverse,
        )
    record_weight = jnp.where(sensor_mask == 1, precision, jnp.zeros_like(precision))
    summed = plain(kernel_spectra, probes, record_weight, fwd_t, inverse)
    numbers = jnp.arange(damping.shape[0], dtype=jnp.int32)
    one_hot = (source_block[:, None] == numbers[None, :]).astype(jnp.float32)
    source_damping = jnp.dot(one_hot, damping, precision=lax.Precision.HIGHEST)
    return summed + source_damping[None, :, None] * probes.astype(jnp.float32)


def solution(mesh):
    placed = (P("row", "col", None), P(None, "row", "col", None), P("row"), P("row"), P("col"), P())
    sizes = (mesh.shape["row"], mesh.shape["col"])
    return jax.shard_map(
        functools.partial(body, sizes),
        mesh=mesh,
        in_specs=placed,
        out_specs=P("row", "col", None),
        check_vma=False,
    )
```

```python
import functools
import math

import jax
import jax.numpy as jnp
import ml_dtypes
import numpy as np
from jax import lax
from jax.experimental import pallas as pl
from jax.experimental.pallas import tpu as pltpu
from jax.sharding import PartitionSpec as P

GROUP = 16
HALVES = 2
DEPTH = 8
LANES = 128
MESH = pl.DeviceIdType.MESH
NT = (((1,), (1,)), ((), ()))
TN = (((0,), (0,)), ((), ()))


def dft_tables(length):
    period = 2 * length
    positions = np.arange(length)
    phases = positions[:, None] * positions[None, :] % period
    angles = phases * (2.0 * math.pi / period)
    cosine = np.cos(angles).astype(np.float32)
    sines = np.sin(angles).astype(np.float32)
    weight = (np.where(positions == 0, 1.0, 2.0) / period).astype(np.float32)
    forward = np.concatenate([cosine, -sines], axis=1).astype(ml_dtypes.bfloat16)
    inverse = np.concatenate([cosine * weight[:, None], -sines * weight[:, None]], axis=0).astype(
        ml_dtypes.bfloat16
    )
    return (forward, inverse)


def dot(a, b, dims=None):
    if dims is None:
        return jnp.dot(a, b, preferred_element_type=jnp.float32)
    return lax.dot_general(a, b, dims, preferred_element_type=jnp.float32)


def fused_kernel(
    n_row,
    n_col,
    halves,
    k_hbm,
    probes_ref,
    mask_ref,
    precision_ref,
    block_ref,
    damping_ref,
    fwd_t_ref,
    inv_ref,
    pick_ref,
    eye_ref,
    out_ref,
    stage,
    kt_first,
    kt_last,
    gath,
    x_ref,
    et_ref,
    pred_ref,
    pred_in,
    wt_ref,
    y_ref,
    acc_ref,
    g_ref,
    wide_even,
    wide_odd,
    pair_out,
    pair_in,
    far_out,
    far_in,
    k_sem,
    gs_sem,
    gr_sem,
    ps_sem,
    pr_sem,
    ws_sem,
    wr_sem,
    hs_sem,
    hr_sem,
    fs_sem,
    fr_sem,
):
    me_row, me_col = lax.axis_index("row"), lax.axis_index("col")
    _, sensors, sources, freqs = k_hbm.shape
    nloc = probes_ref.shape[0]
    nprobe = nloc * n_row
    nown = nprobe // n_col
    groups = freqs // GROUP
    columns = nprobe * 2 * GROUP
    depth, _, rows, _, _ = stage.shape
    steps = sensors // rows
    half = sensors // halves
    kts = [kt_first, kt_last]

    def row_peer(d):
        return lax.rem(me_row + d, n_row)

    def col_peer(d):
        return lax.rem(me_col + d, n_col)

    def load(step, slot):
        at = pl.ds(pl.multiple_of(step * rows, rows), rows)
        return pltpu.make_async_copy(k_hbm.at[:, at], stage.at[slot], k_sem.at[slot])

    for slot in range(depth):
        load(slot, slot).start()

    barrier = pltpu.get_barrier_semaphore()
    for d in range(1, n_row):
        pl.semaphore_signal(barrier, inc=1, device_id=(row_peer(d), me_col), device_id_type=MESH)
    for d in range(1, n_col):
        pl.semaphore_signal(barrier, inc=1, device_id=(me_row, col_peer(d)), device_id_type=MESH)
    pl.semaphore_wait(barrier, n_row + n_col - 2)

    def send(src, dst, send_sem, recv_sem, device):
        return pltpu.make_async_remote_copy(
            src_ref=src,
            dst_ref=dst,
            send_sem=send_sem,
            recv_sem=recv_sem,
            device_id=device,
            device_id_type=MESH,
        )

    gathers = []
    for d in range(1, n_row):
        copy = send(
            probes_ref,
            gath.at[d],
            gs_sem.at[d],
            gr_sem.at[d],
            (row_peer(d), me_col),
        )
        copy.start()
        gathers.append(copy)

    def turn(kt, slot, r, row):
        real = stage[slot, 0, r].T
        imag = dot(eye_ref[...], stage[slot, 1, r], NT).astype(jnp.bfloat16)
        kt[:, 0, row, :, :] = real.reshape(groups, GROUP, sources)
        kt[:, 1, row, :, :] = imag.reshape(groups, GROUP, sources)

    def load_next(step, slot):
        @pl.when(step + depth < steps)
        def _():
            load(step + depth, slot).start()

    def turn_first(step, carry):
        slot = lax.rem(step, depth)
        load(step, slot).wait()
        for r in range(rows):
            turn(kt_first, slot, r, step * rows + r)
        load_next(step, slot)
        return carry

    lax.fori_loop(0, groups, turn_first, 0)

    def spectra(p, block):
        spec = dot(fwd_t_ref[...], block, NT).astype(jnp.bfloat16)
        real = spec[:freqs].reshape(groups, GROUP, sources)
        imag = spec[freqs:].reshape(groups, GROUP, sources)
        first = pl.ds(pl.multiple_of(p * 2 * GROUP, GROUP), GROUP)
        second = pl.ds(pl.multiple_of(p * 2 * GROUP + GROUP, GROUP), GROUP)
        x_ref[:, first, :sources] = real
        x_ref[:, second, :sources] = imag
        x_ref[:, first, sources:] = -imag
        x_ref[:, second, sources:] = real

    for j in range(nloc):
        spectra(me_row * nloc + j, probes_ref[j])
    for d in range(1, n_row):
        gathers[d - 1].wait_recv()
        origin = lax.rem(me_row + n_row - d, n_row)
        for j in range(nloc):
            spectra(origin * nloc + j, gath[d, j])

    def column(row, width):
        tall = jnp.broadcast_to(row, (LANES, row.shape[1])).T
        return jnp.concatenate([tall] * (width // LANES), axis=1)

    times = probes_ref.shape[2]
    precision = precision_ref[...]
    sensor_weight = column(
        jnp.where(mask_ref[...] == 1, precision, jnp.zeros_like(precision)), times
    )

    own = lax.broadcasted_iota(jnp.int32, (1, GROUP, columns), 1)
    col = lax.broadcasted_iota(jnp.int32, (1, GROUP, columns), 2) % GROUP
    keep = own == col
    own = lax.broadcasted_iota(jnp.int32, (1, GROUP, half * GROUP), 1)
    col = lax.broadcasted_iota(jnp.int32, (1, GROUP, half * GROUP), 2) % GROUP
    keep_wide = own == col

    def forward_chunk(h, g, first, count):
        left = [
            kts[h][g, k, first : first + count].reshape(count * GROUP, sources) for k in range(2)
        ]
        out = dot(jnp.concatenate(left, axis=1), x_ref[g], NT)
        kept = jnp.where(keep, out.reshape(count, GROUP, columns), 0.0).astype(jnp.bfloat16)
        return dot(pick_ref[:count, : count * GROUP], kept.reshape(count * GROUP, columns))

    def store_blocks(g, block):
        et_ref[:, :, g] = block.T.astype(jnp.bfloat16).reshape(nprobe, 2, GROUP, half)

    def forward_turning(g, carry):
        step = groups + g
        slot = lax.rem(step, depth)
        load(step, slot).wait()
        count = half // 2
        blocks = []
        for piece in range(2):
            for r in range(piece * rows // 2, (piece + 1) * rows // 2):
                turn(kt_last, slot, r, g * rows + r)
            blocks.append(forward_chunk(0, g, piece * count, count))
        store_blocks(g, jnp.concatenate(blocks, axis=0))
        load_next(step, slot)
        return carry

    def forward_part(h, low, high):
        def one(g, carry):
            store_blocks(g, forward_chunk(h, g, 0, half))
            return carry

        lax.fori_loop(low, high, one, 0, unroll=2)

    sends = []

    def predict(h):
        for p in range(nprobe):
            spec = et_ref[p].reshape(2 * freqs, half)
            pred_ref[h, p // nown, p % nown] = dot(spec, inv_ref[...], TN).astype(jnp.bfloat16)
        copies = []
        for d in range(1, n_col):
            copy = send(
                pred_ref.at[h, col_peer(d)],
                pred_in.at[h, d - 1],
                ps_sem.at[h, d - 1],
                pr_sem.at[h, d - 1],
                (me_row, col_peer(d)),
            )
            copy.start()
            copies.append(copy)
        sends.extend(copies)
        return copies

    def weigh(h, copies):
        total = pred_ref[h, me_col].astype(jnp.float32)
        for d in range(1, n_col):
            copies[d - 1].wait_recv()
            total = total + pred_in[h, d - 1].astype(jnp.float32)
        scale = sensor_weight[h * half : (h + 1) * half]
        wt_ref[h, me_col] = (total * scale[None]).astype(jnp.bfloat16)
        out = []
        for d in range(1, n_col):
            copy = send(
                wt_ref.at[h, me_col],
                wt_ref.at[h, me_col],
                ws_sem.at[h, d - 1],
                wr_sem.at[h, d - 1],
                (me_row, col_peer(d)),
            )
            copy.start()
            out.append(copy)
        sends.extend(out)
        return out

    def residual(h, copies):
        for copy in copies:
            copy.wait_recv()
        for p in range(nprobe):
            spec = dot(inv_ref[...], wt_ref[h, p // nown, p % nown], NT).astype(jnp.bfloat16)
            for k in range(2):
                at = (2 * p + k) * GROUP
                y_ref[:, at : at + GROUP, :] = spec[k * freqs : (k + 1) * freqs].reshape(
                    groups, GROUP, half
                )

    def widen(g, wide_ref):
        wide = dot(y_ref[g], pick_ref[...]).reshape(2 * nprobe, GROUP, half * GROUP)
        wide = jnp.where(keep_wide, wide, 0.0).astype(jnp.bfloat16)
        wide_ref[...] = wide.reshape(columns, half * GROUP)

    def multiply(h, g, wide_ref):
        both = [
            dot(wide_ref[...], kts[h][g, k].reshape(half * GROUP, sources)).reshape(
                nprobe, 2, GROUP, sources
            )
            for k in range(2)
        ]
        real = both[0][:, 0] + both[1][:, 1]
        imag = both[0][:, 1] - both[1][:, 0]
        if h > 0:
            real = real + acc_ref[g, 0]
            imag = imag + acc_ref[g, 1]
        if h < halves - 1:
            acc_ref[g, 0] = real
            acc_ref[g, 1] = imag
        else:
            g_ref[:, 0, g] = real.astype(jnp.bfloat16)
            g_ref[:, 1, g] = imag.astype(jnp.bfloat16)

    def adjoint_part(h, low, high):
        widen(low, wide_even)

        def two(i, carry):
            g = low + 2 * i
            widen(g + 1, wide_odd)
            multiply(h, g, wide_even)
            widen(lax.rem(g + 2, groups), wide_even)
            multiply(h, g + 1, wide_odd)
            return carry

        lax.fori_loop(0, (high - low) // 2, two, 0)

    mid = groups // 2
    lax.fori_loop(0, groups, forward_turning, 0)
    pred_copies = predict(0)
    for h in range(1, halves):
        forward_part(h, 0, mid)
        wt_copies = weigh(h - 1, pred_copies)
        forward_part(h, mid, groups)
        pred_copies = predict(h)
        residual(h - 1, wt_copies)
        adjoint_part(h - 1, 0, mid)
        wt_copies = weigh(h, pred_copies)
        adjoint_part(h - 1, mid, groups)
    residual(halves - 1, wt_copies)
    adjoint_part(halves - 1, 0, groups)

    def history(p):
        return dot(g_ref[p].reshape(2 * freqs, sources), fwd_t_ref[...], TN)

    def flip(change):
        place, bit = 0, 1
        while bit < n_row:
            place = place + lax.rem(lax.div(me_row, bit) + (change // bit) % 2, 2) * bit
            bit *= 2
        return place

    changes = list(range(n_row - 2, -1, -2))
    backs, joins = [], []
    for i, change in enumerate(changes):
        peer = flip(change + 1)
        for j in range(nloc):
            pair_out[i, j] = history(peer * nloc + j).astype(jnp.bfloat16)
        copy = send(
            pair_out.at[i], pair_in.at[i], hs_sem.at[i], hr_sem.at[i], (flip(1), me_col)
        )
        copy.start()
        joins.append(copy)
    for i, change in enumerate(changes):
        peer = flip(change)
        total = [history(peer * nloc + j) for j in range(nloc)]
        joins[i].wait_recv()
        total = [total[j] + pair_in[i, j].astype(jnp.float32) for j in range(nloc)]
        if change > 0:
            for j in range(nloc):
                far_out[i, j] = total[j].astype(jnp.bfloat16)
            copy = send(
                far_out.at[i], far_in.at[i], fs_sem.at[i], fr_sem.at[i], (peer, me_col)
            )
            copy.start()
            backs.append(copy)
    group_of = block_ref[...]
    damp = jnp.zeros(group_of.shape, jnp.float32)
    for n in range(damping_ref.shape[0]):
        damp = jnp.where(group_of == n, damping_ref[n], damp)
    damp = column(damp, times)
    for j in range(nloc):
        out_ref[j] = total[j] + damp * probes_ref[j].astype(jnp.float32)
    for i, copy in enumerate(backs):
        copy.wait_recv()
        for j in range(nloc):
            out_ref[j] += far_in[i, j].astype(jnp.float32)
    for copy in gathers + sends + joins + backs:
        copy.wait_send()


def fused_call(
    mesh_sizes,
    kernel_spectra,
    probes,
    sensor_mask,
    precision,
    source_block,
    damping,
    fwd_t,
    inverse,
):
    n_row, n_col = mesh_sizes
    _, sensors, sources, freqs = kernel_spectra.shape
    nloc, _, times = probes.shape
    nprobe = nloc * n_row
    nown = nprobe // n_col
    groups = freqs // GROUP
    columns = nprobe * 2 * GROUP
    halves = HALVES
    half = sensors // halves
    rows = half // groups
    owner = np.arange(half * GROUP)[None, :] // GROUP
    pick = jnp.asarray((np.arange(half)[:, None] == owner).astype(ml_dtypes.bfloat16))
    vmem = pl.BlockSpec(memory_space=pltpu.VMEM)
    low = jnp.bfloat16
    dma = pltpu.SemaphoreType.DMA
    return pl.pallas_call(
        functools.partial(fused_kernel, n_row, n_col, halves),
        in_specs=[pl.BlockSpec(memory_space=pl.ANY)]
        + [vmem] * 4
        + [pl.BlockSpec(memory_space=pltpu.SMEM)]
        + [vmem] * 4,
        out_specs=vmem,
        out_shape=jax.ShapeDtypeStruct(probes.shape, jnp.float32),
        scratch_shapes=[
            pltpu.VMEM((DEPTH, 2, rows, sources, freqs), low),
            pltpu.VMEM((groups, 2, half, GROUP, sources), low),
            pltpu.VMEM((groups, 2, half, GROUP, sources), low),
            pltpu.VMEM((n_row,) + probes.shape, low),
            pltpu.VMEM((groups, columns, 2 * sources), low),
            pltpu.VMEM((nprobe, 2, groups, GROUP, half), low),
            pltpu.VMEM((halves, n_col, nown, half, times), low),
            pltpu.VMEM((halves, n_col - 1, nown, half, times), low),
            pltpu.VMEM((halves, n_col, nown, half, times), low),
            pltpu.VMEM((groups, columns, half), low),
            pltpu.VMEM((groups, 2, nprobe, GROUP, sources), jnp.float32),
            pltpu.VMEM((nprobe, 2, groups, GROUP, sources), low),
            pltpu.VMEM((columns, half * GROUP), low),
            pltpu.VMEM((columns, half * GROUP), low),
            pltpu.VMEM((n_row // 2,) + probes.shape, low),
            pltpu.VMEM((n_row // 2,) + probes.shape, low),
            pltpu.VMEM((n_row // 2 - 1,) + probes.shape, low),
            pltpu.VMEM((n_row // 2 - 1,) + probes.shape, low),
            dma((DEPTH,)),
            dma((n_row,)),
            dma((n_row,)),
            dma((halves, n_col - 1)),
            dma((halves, n_col - 1)),
            dma((halves, n_col - 1)),
            dma((halves, n_col - 1)),
            dma((n_row // 2,)),
            dma((n_row // 2,)),
            dma((n_row // 2 - 1,)),
            dma((n_row // 2 - 1,)),
        ],
        compiler_params=pltpu.CompilerParams(
            vmem_limit_bytes=60 * 1024 * 1024, collective_id=0, has_side_effects=True
        ),
        name="fused",
    )(
        kernel_spectra,
        probes,
        sensor_mask[None, :],
        precision[None, :],
        source_block[None, :],
        damping,
        fwd_t,
        inverse,
        pick,
        jnp.asarray(np.eye(freqs).astype(ml_dtypes.bfloat16)),
    )


def plain_forward(kernel_spectra, probes, fwd_t, inv_t):
    freqs = kernel_spectra.shape[3]
    spec = jnp.einsum("Ft,pst->psF", fwd_t, probes, preferred_element_type=jnp.float32)
    spec = spec.astype(jnp.bfloat16)
    spec = spec.reshape(spec.shape[:2] + (2, freqs))
    a = jnp.einsum("krsf,psjf->kjprf", kernel_spectra, spec, preferred_element_type=jnp.float32)
    both = jnp.concatenate([a[0, 0] - a[1, 1], a[0, 1] + a[1, 0]], axis=-1).astype(jnp.bfloat16)
    pred = jnp.einsum("tF,prF->ptr", inv_t, both, preferred_element_type=jnp.float32)
    return kernel_spectra, pred.astype(jnp.bfloat16)


def plain_adjoint(kernel_spectra, weighted, inverse, synthesis):
    freqs = kernel_spectra.shape[3]
    spec = jnp.einsum("Ft,ptr->prF", inverse, weighted, preferred_element_type=jnp.float32)
    spec = spec.astype(jnp.bfloat16)
    spec = spec.reshape(spec.shape[:2] + (2, freqs))
    a = jnp.einsum("krsf,prjf->kjpsf", kernel_spectra, spec, preferred_element_type=jnp.float32)
    both = jnp.concatenate([a[0, 0] + a[1, 1], a[0, 1] - a[1, 0]], axis=-1).astype(jnp.bfloat16)
    out = jnp.einsum("psF,Ft->pst", both, synthesis, preferred_element_type=jnp.float32)
    return out.astype(jnp.bfloat16)


def plain(kernel_spectra, probes, record_weight, fwd_t, inverse):
    gathered = lax.all_gather(probes, "row", axis=0, tiled=True)
    turned, pred = plain_forward(kernel_spectra, gathered, fwd_t, inverse.T)
    predicted = lax.psum_scatter(pred, "col", scatter_dimension=0, tiled=True)
    weighted = (predicted.astype(jnp.float32) * record_weight[None, None, :]).astype(jnp.bfloat16)
    weighted = lax.all_gather(weighted, "col", axis=0, tiled=True)
    part = plain_adjoint(turned, weighted, inverse, fwd_t)
    return lax.psum_scatter(part, "row", scatter_dimension=0, tiled=True).astype(jnp.float32)


def body(sizes, probes, kernel_spectra, sensor_mask, precision, source_block, damping):
    forward, inverse = dft_tables(probes.shape[2])
    fwd_t, inverse = jnp.asarray(forward.T), jnp.asarray(inverse)
    _, sensors, sources, freqs = kernel_spectra.shape
    half, groups = sensors // HALVES, freqs // GROUP
    aligned = all(size % LANES == 0 for size in (sensors, sources, freqs))
    paired = sizes[0] >= 4 and sizes[0] & (sizes[0] - 1) == 0
    if aligned and paired and half % (2 * groups) == 0 and sensors // (half // groups) >= DEPTH:
        return fused_call(
            sizes,
            kernel_spectra,
            probes,
            sensor_mask,
            precision,
            source_block,
            damping,
            fwd_t,
            inverse,
        )
    record_weight = jnp.where(sensor_mask == 1, precision, jnp.zeros_like(precision))
    summed = plain(kernel_spectra, probes, record_weight, fwd_t, inverse)
    numbers = jnp.arange(damping.shape[0], dtype=jnp.int32)
    one_hot = (source_block[:, None] == numbers[None, :]).astype(jnp.float32)
    source_damping = jnp.dot(one_hot, damping, precision=lax.Precision.HIGHEST)
    return summed + source_damping[None, :, None] * probes.astype(jnp.float32)


def solution(mesh):
    placed = (P("row", "col", None), P(None, "row", "col", None), P("row"), P("row"), P("col"), P())
    sizes = (mesh.shape["row"], mesh.shape["col"])
    return jax.shard_map(
        functools.partial(body, sizes),
        mesh=mesh,
        in_specs=placed,
        out_specs=P("row", "col", None),
        check_vma=False,
    )
```
